512 devices in a mesh: dp: 64 (over z_lo, y, core), tensor: 8 (over x, z_hi).
Axes of the slice: x: 4, y: 8, z: 8 (z_hi: 2, z_lo: 4; z = z_hi * 4 + z_lo), core: 2. Of those that a mesh axis runs over, the one named last changes fastest.
Arguments:
- tokens: bfloat16 [16384, 2560], P('dp', 'tensor'), may hold values from -6 to 6
- gate_weight: bfloat16 [40960, 6912], P('dp', 'tensor'), may hold values from -0.125 to 0.125
- up_weight: bfloat16 [40960, 6912], P('dp', 'tensor'), may hold values from -0.125 to 0.125
- hidden_grad: bfloat16 [16384, 6912], P('dp', 'tensor'), may hold values from -6 to 6
- step_index: int32 [1], replicated, may hold values from 0 to 999
Outputs:
- averaged_up: bfloat16 [40960, 6912], P('dp', 'tensor')
- input_grad: bfloat16 [16384, 2560], P('dp', 'tensor')
The draws below stay inside these ranges and needn't reach their ends.
All inputs are finite; a program needn't handle non-finite values.
Results may differ from the reference program's by a relative error of at most 0.013.
Values may be sent and summed in bfloat16 or wider, within the bound.
A program may use at most 128 MiB of HBM per device.

```python
import jax
import jax.numpy as jnp
from jax import lax

D = 2560
FF = 6912
TOK_DEV = 256
GROUPS = 16
TOKENS = 16384


def steps_of(rng, shape, cuts, smallest, largest):
    factor_of, own = 1.0, jax.random.fold_in(rng, 6)
    for axis_at, blocks in cuts:
        draws = jnp.exp(jax.random.uniform(jax.random.fold_in(own, axis_at), (blocks,), jnp.float32, smallest / len(cuts), largest / len(cuts)))
        factor_of = factor_of * jnp.repeat(draws, shape[axis_at] // blocks).reshape([-1 if axis == axis_at else 1 for axis in range(len(shape))])
    return factor_of


def centred(stream_key, shape, deviation, limit, split=(), held_as=jnp.bfloat16):
    result = jax.random.normal(stream_key, shape, jnp.float32) * deviation
    if len(split) > 0:
        result = steps_of(stream_key, shape, split, -0.22, 0.18) * result
    return jnp.clip(result, min=-limit, max=limit).astype(held_as)


def setup_inputs(seed: int = 0) -> dict:
    splits = jax.random.split(jax.random.key(seed), 6)
    tokens = centred(splits[0], (TOKENS, D), 1.0, 6.0, ((0, 64), (1, 8)))
    gate_weight = centred(splits[1], (GROUPS * D, FF), D ** -0.5, 0.125, ((0, 64), (1, 8)))
    up_weight = centred(splits[2], (GROUPS * D, FF), D ** -0.5, 0.125, ((0, 64), (1, 8)))
    hidden_grad = centred(splits[3], (TOKENS, FF), 1.0, 6.0, ((0, 64), (1, 8)))
    step_index = jax.random.randint(splits[4], (1,), 0, 1000).astype(jnp.int32)
    return dict(tokens=tokens, gate_weight=gate_weight, up_weight=up_weight, hidden_grad=hidden_grad, step_index=step_index)


def group_step(x_g, gate_w, up_w, cot):
    gate = jnp.dot(x_g, gate_w, preferred_element_type=jnp.float32)
    up = jnp.dot(x_g, up_w, preferred_element_type=jnp.float32)
    sig = jax.nn.sigmoid(gate)
    cot_wide = cot.astype(jnp.float32)
    up_delta = (cot_wide * gate * sig).astype(jnp.bfloat16)
    gate_delta = (cot_wide * up * sig * (1.0 + gate * (1.0 - sig))).astype(jnp.bfloat16)
    grad_in = jnp.dot(up_delta, up_w.T, preferred_element_type=jnp.float32) + jnp.dot(gate_delta, gate_w.T, preferred_element_type=jnp.float32)
    up_grad = jnp.dot(x_g.T, up_delta, preferred_element_type=jnp.float32)
    stepped = (up_w.astype(jnp.float32) - 0.002 * up_grad).astype(jnp.bfloat16)
    return stepped, grad_in.astype(jnp.bfloat16)


def reference(tokens, gate_weight, up_weight, hidden_grad, step_index):
    rows = 4 * TOK_DEV
    x_all = tokens.reshape(GROUPS, rows, D)
    gate_all = gate_weight.reshape(GROUPS, D, FF)
    up_all = up_weight.reshape(GROUPS, D, FF)
    cot_all = hidden_grad.reshape(GROUPS, rows, FF)

    def one(pieces):
        return group_step(pieces[0], pieces[1], pieces[2], pieces[3])

    stepped, grad_in = lax.map(one, (x_all, gate_all, up_all, cot_all))
    levels = GROUPS.bit_length() - 1
    power = jnp.left_shift(jnp.int32(1), (step_index[0] % levels).astype(jnp.int32))
    peer = jnp.roll(stepped, power, axis=0)
    averaged = ((stepped.astype(jnp.float32) + peer.astype(jnp.float32)) * 0.5).astype(jnp.bfloat16)
    return averaged.reshape(GROUPS * D, FF), grad_in.reshape(TOKENS, D)
```

```python
import functools

import jax
import jax.numpy as jnp
from jax import lax
from jax.experimental import pallas as pl
from jax.experimental.pallas import tpu as pltpu
from jax.sharding import PartitionSpec as P

MESH = pl.DeviceIdType.MESH
BF16, F32 = jnp.bfloat16, jnp.float32
WIDE = 256

X_Z, X_Y, X_FAR, X_NEAR = 0, 1, 3, 7
W_CORE, COT, X_CORE, PART, DELTA, STEP = 11, 13, 14, 15, 19, 23
G_NEAR, G_FAR, G_Y, G_Z, SENDS = 27, 31, 35, 37, 38
X_IN = 0
R_W, R_COT, R_XC, R_PART, R_DELTA, R_STEP = 9, 11, 12, 13, 17, 21
R_NEAR, R_FAR, R_Y, R_Z, RECVS = 25, 29, 33, 35, 36


def step_kernel(
    level, groups_dp, tok, gw, uw, cot, avg_ref, ig_ref,
    xin, xr, xs, xt, wgb, wub, hg,
    pf_m, pf_t, sb_m, sb_t, rb_m, rb_t, ud_m, ud_t, us_m, us_t, gd_m, gd_t,
    st_m, st_t, pr_m, pr_t, acc, near_out, near_in, far_out, far_in, y_out, y_in, z_out, z_in,
    avg_buf, ig_buf, snd, rcv, loc,
):
    T, F = tok.shape
    R, C = gw.shape
    full = C // WIDE
    rest = C - full * WIDE
    dp, t = lax.axis_index("dp"), lax.axis_index("tensor")
    core, side = lax.rem(dp, 2), lax.rem(dp // 2, 2)
    x, zh = t // 2, lax.rem(t, 2)
    place = lax.rem(x - 2 * side + 4, 4)
    home = place < 2
    away = place >= 2
    odd = lax.rem(place, 2)
    prim = jnp.where(home, odd, 1 - odd)
    xbit = lax.rem(x, 2)

    sibling = (dp + 1 - 2 * core, t)
    across = (dp + 2 - 4 * side, t)
    anti = (dp, t + 1 - 2 * zh)
    near = (dp, (x + 1 - 2 * xbit) * 2 + zh)
    far = (dp, lax.rem(2 * side + 3 - place, 4) * 2 + zh)
    shift = 4 * 2**level
    target = (lax.rem(dp + shift, groups_dp), t)
    origin = (lax.rem(dp + groups_dp - shift, groups_dp), t)

    partners = [sibling, across, anti, near, far, target]
    if 2 * shift != groups_dp:
        partners.append(origin)
    barrier = pltpu.get_barrier_semaphore()
    for partner in partners:
        pl.semaphore_signal(barrier, inc=1, device_id=partner, device_id_type=MESH)
    pl.semaphore_wait(barrier, len(partners))

    def remote(src, dst, s, r, device):
        return pltpu.make_async_remote_copy(
            src_ref=src, dst_ref=dst, send_sem=snd.at[s], recv_sem=rcv.at[r],
            device_id=device, device_id_type=MESH,
        )

    def slot(i, z, y):
        return (i * 2 + z) * 2 + y

    blocks = [(zh, side), (zh, 1 - side), (1 - zh, side), (1 - zh, 1 - side)]

    def to_x(n, src, which, device):
        index = slot(prim, *blocks[n])
        return remote(src, xin.at[index], which + n, X_IN + index, device)

    def arrived(index):
        remote(tok, xin.at[index], X_Z, X_IN + index, anti).wait_recv()

    z_slot = jnp.where(home, slot(xbit, zh, side), 8)
    z_in_slot = jnp.where(home, slot(xbit, 1 - zh, side), 8)
    z_copy = remote(tok, xin.at[z_slot], X_Z, X_IN + z_slot, anti)
    y_first, y_second = slot(xbit, zh, side), slot(xbit, 1 - zh, side)
    y_own = remote(tok, xin.at[y_first], X_Y, X_IN + y_first, across)
    y_anti = remote(xin.at[8], xin.at[y_second], X_Y + 1, X_IN + y_second, across)
    own_x = pltpu.make_async_copy(tok, xin.at[slot(xbit, zh, side)], loc.at[0])
    cot_copy = remote(cot, hg.at[side], COT, R_COT, across)
    z_copy.start()

    @pl.when(home)
    def _():
        own_x.start()
        to_x(0, tok, X_FAR, far).start()
        to_x(0, tok, X_NEAR, near).start()
        cot_copy.start()

    @pl.when(away)
    def _():
        y_own.start()

    w_copies = [
        remote(gw, wgb.at[core], W_CORE, R_W, sibling),
        remote(uw, wub.at[core], W_CORE + 1, R_W + 1, sibling),
    ]
    own_copies = [
        pltpu.make_async_copy(gw, wgb.at[core], loc.at[1]),
        pltpu.make_async_copy(uw, wub.at[core], loc.at[2]),
        pltpu.make_async_copy(cot, hg.at[side], loc.at[3]),
    ]
    for copy in own_copies + w_copies:
        copy.start()

    @pl.when(home)
    def _():
        for n in (1, 2, 3):
            index = slot(prim, *blocks[n])
            arrived(index)
            to_x(n, xin.at[index], X_FAR, far).start()
            to_x(n, xin.at[index], X_NEAR, near).start()
        own_x.wait()

    @pl.when(away)
    def _():
        for n in range(4):
            if n == 1:
                arrived(z_in_slot)
                y_anti.start()
                cot_copy.start()
            index = slot(prim, *blocks[n])
            arrived(index)
            to_x(n, xin.at[index], X_FAR, near).start()

    acc[...] = jnp.zeros_like(acc)
    for n in range(4):
        arrived(slot(1 - prim, *blocks[n]))
    for i in range(2):
        for y in range(2):
            xr[i, y * T : (y + 1) * T, :] = jnp.concatenate(
                [xin[slot(i, 0, y)], xin[slot(i, 1, y)]], axis=1
            )
    x_copy = remote(xr.at[1 - core], xs, X_CORE, R_XC, sibling)
    x_copy.start()
    for copy in own_copies:
        copy.wait()
    for copy in w_copies:
        copy.wait_recv()

    class Part:
        def __init__(self, j, main):
            pick = (lambda a, b: a.at[j]) if main else (lambda a, b: b)
            self.width = WIDE if main else rest
            start = pl.multiple_of(j * WIDE, WIDE) if main else full * WIDE
            self.columns = pl.ds(start, self.width)
            self.pf, self.sb, self.rb = pick(pf_m, pf_t), pick(sb_m, sb_t), pick(rb_m, rb_t)
            self.ud, self.us, self.gd = pick(ud_m, ud_t), pick(us_m, us_t), pick(gd_m, gd_t)
            self.st, self.pr = pick(st_m, st_t), pick(pr_m, pr_t)
            self.j = j

        def sums(self):
            return remote(self.sb, self.rb, PART + self.j, R_PART + self.j, across)

        def deltas(self):
            return remote(self.ud, self.us, DELTA + self.j, R_DELTA + self.j, sibling)

        def peer(self):
            return remote(self.st, self.pr, STEP + self.j, R_STEP + self.j, target)

    def each_part(body):
        @pl.loop(0, full)
        def _(j):
            body(Part(j, True))

        if rest:
            body(Part(full, False))

    def rows_of(r, size):
        return pl.ds(pl.multiple_of(r * size, size), size)

    def sums(part):
        @pl.loop(0, 2)
        def _(r):
            rows = rows_of(r, T)
            for n, w in ((0, wgb), (1, wub)):
                total = jnp.dot(
                    xr[0, rows, :], w[0, :, part.columns], preferred_element_type=F32
                ) + jnp.dot(xr[1, rows, :], w[1, :, part.columns], preferred_element_type=F32)
                part.pf[n, rows, :] = total
                part.sb[n, rows, :] = total.astype(BF16)

        part.sums().start()

    each_part(sums)

    xt[:, : 2 * T] = xr[core].T
    x_copy.wait_recv()
    xt[:, 2 * T :] = xs[...].T
    cot_copy.wait_recv()

    tile = 64 if T % 64 == 0 else T

    def deltas(part):
        part.sums().wait_recv()
        for y in range(2):

            @pl.loop(0, T // tile)
            def _(r):
                rows = pl.ds(pl.multiple_of(y * T + r * tile, tile), tile)
                gate = part.pf[0, rows, :] + part.rb[0, rows, :].astype(F32)
                up = part.pf[1, rows, :] + part.rb[1, rows, :].astype(F32)
                sig = 1.0 / (1.0 + jnp.exp(-gate))
                wide = hg[y, rows_of(r, tile), part.columns].astype(F32)
                part.ud[rows, :] = (wide * gate * sig).astype(BF16)
                part.gd[rows, :] = (wide * up * sig * (1.0 + gate * (1.0 - sig))).astype(BF16)

        part.deltas().start()

        @pl.loop(0, 2)
        def _(r):
            rows = rows_of(r, T)
            for i in range(2):
                acc[i, rows, :] += lax.dot_general(
                    part.ud[rows, :], wub[i, :, part.columns], (((1,), (1,)), ((), ())),
                    preferred_element_type=F32,
                ) + lax.dot_general(
                    part.gd[rows, :], wgb[i, :, part.columns], (((1,), (1,)), ((), ())),
                    preferred_element_type=F32,
                )

        part.deltas().wait_recv()

        @pl.loop(0, R // 128)
        def _(r):
            rows = rows_of(r, 128)
            grad = jnp.dot(xt[rows, : 2 * T], part.ud[...], preferred_element_type=F32) + jnp.dot(
                xt[rows, 2 * T :], part.us[...], preferred_element_type=F32
            )
            old = wub[core, rows, part.columns].astype(F32)
            part.st[rows, :] = (old - 0.002 * grad).astype(BF16)

        part.peer().start()

    each_part(deltas)

    H = T // 2
    pieces = [(1 - side, 0), (1 - side, 1), (side, 0), (side, 1)]

    def piece_rows(n):
        y, half = pieces[n]
        return pl.ds(pl.multiple_of(y * T + half * H, H), H)

    def g_near(n):
        return remote(near_out.at[n], near_in.at[n], G_NEAR + n, R_NEAR + n, near)

    def g_far(n):
        return remote(far_out.at[n], far_in.at[n], G_FAR + n, R_FAR + n, far)

    def g_y(half):
        return remote(y_out.at[half], y_in.at[half], G_Y + half, R_Y + half, across)

    for n in range(4):
        near_out[n] = acc[1 - prim, piece_rows(n), :].astype(BF16)
        g_near(n).start()

    @pl.when(away)
    def _():
        for n in range(4):
            g_near(n).wait_recv()
            far_out[n] = (
                acc[prim, piece_rows(n), :] + near_in[n].astype(F32)
            ).astype(BF16)
            g_far(n).start()

    def at_home(n):
        g_near(n).wait_recv()
        g_far(n).wait_recv()
        return (
            acc[prim, piece_rows(n), :] + near_in[n].astype(F32) + far_in[n].astype(F32)
        )

    mine = acc.at[prim]
    own = pl.ds(pl.multiple_of(side * T, T), T)

    @pl.when(home)
    def _():
        for n in range(2):
            y_out[n] = at_home(n).astype(BF16)
            g_y(n).start()
        for n in range(2, 4):
            mine[piece_rows(n), :] = at_home(n)

    @pl.when(away)
    def _():
        for n in range(2):
            g_y(n).wait_recv()
            mine[piece_rows(n + 2), :] = y_in[n].astype(F32)

    total = mine[own, :]
    low, high = total[:, :F], total[:, F:]
    z_out[...] = jnp.where(zh == 0, high, low).astype(BF16)
    g_z = remote(z_out, z_in, G_Z, R_Z, anti)
    g_z.start()
    g_z.wait_recv()
    ig_buf[...] = (jnp.where(zh == 0, low, high) + z_in[...].astype(F32)).astype(BF16)
    ig_copy = pltpu.make_async_copy(ig_buf, ig_ref, loc.at[4])
    ig_copy.start()

    def average(part):
        part.peer().wait_recv()
        avg_buf[:, part.columns] = (
            (part.st[...].astype(F32) + part.pr[...].astype(F32)) * 0.5
        ).astype(BF16)

    each_part(average)
    avg_copy = pltpu.make_async_copy(avg_buf, avg_ref, loc.at[5])
    avg_copy.start()

    z_copy.wait_send()
    cot_copy.wait_send()
    x_copy.wait_send()
    for copy in w_copies:
        copy.wait_send()
    for n in range(4):
        to_x(n, tok, X_FAR, far).wait_send()
        g_near(n).wait_send()

    @pl.when(home)
    def _():
        for n in range(4):
            to_x(n, tok, X_NEAR, near).wait_send()
        for n in range(2):
            g_y(n).wait_send()

    @pl.when(away)
    def _():
        y_own.wait_send()
        y_anti.wait_send()
        for n in range(4):
            g_far(n).wait_send()

    def left(part):
        part.sums().wait_send()
        part.deltas().wait_send()
        part.peer().wait_send()

    each_part(left)
    g_z.wait_send()
    ig_copy.wait()
    avg_copy.wait()


def call_step(level, groups_dp, tokens, gate_weight, up_weight, hidden_grad):
    T, F = tokens.shape
    R, C = gate_weight.shape
    full = C // WIDE
    rest = C - full * WIDE

    def both(shape, kind):
        return [
            pltpu.VMEM((full, *shape, WIDE), kind),
            pltpu.VMEM((*shape, rest), kind),
        ]

    scratch = [
        pltpu.VMEM((9, T, F), BF16),
        pltpu.VMEM((2, 2 * T, R), BF16),
        pltpu.VMEM((2 * T, R), BF16),
        pltpu.VMEM((R, 4 * T), BF16),
        pltpu.VMEM((2, R, C), BF16),
        pltpu.VMEM((2, R, C), BF16),
        pltpu.VMEM((2, T, C), BF16),
        *both((2, 2 * T), F32),
        *both((2, 2 * T), BF16),
        *both((2, 2 * T), BF16),
        *both((2 * T,), BF16),
        *both((2 * T,), BF16),
        *both((2 * T,), BF16),
        *both((R,), BF16),
        *both((R,), BF16),
        pltpu.VMEM((2, 2 * T, R), F32),
        pltpu.VMEM((4, T // 2, R), BF16),
        pltpu.VMEM((4, T // 2, R), BF16),
        pltpu.VMEM((4, T // 2, R), BF16),
        pltpu.VMEM((4, T // 2, R), BF16),
        pltpu.VMEM((2, T // 2, R), BF16),
        pltpu.VMEM((2, T // 2, R), BF16),
        pltpu.VMEM((T, F), BF16),
        pltpu.VMEM((T, F), BF16),
        pltpu.VMEM((R, C), BF16),
        pltpu.VMEM((T, F), BF16),
        pltpu.SemaphoreType.DMA((SENDS,)),
        pltpu.SemaphoreType.DMA((RECVS,)),
        pltpu.SemaphoreType.DMA((6,)),
    ]
    return pl.pallas_call(
        functools.partial(step_kernel, level, groups_dp),
        out_shape=(
            jax.ShapeDtypeStruct((R, C), BF16),
            jax.ShapeDtypeStruct((T, F), BF16),
        ),
        in_specs=[pl.BlockSpec(memory_space=pl.ANY)] * 4,
        out_specs=[pl.BlockSpec(memory_space=pl.ANY)] * 2,
        scratch_shapes=scratch,
        compiler_params=pltpu.CompilerParams(
            collective_id=level, has_side_effects=True, vmem_limit_bytes=56 * 2**20
        ),
        cost_estimate=pl.CostEstimate(
            flops=20 * T * 8 * F * C, bytes_accessed=6 * R * C, transcendentals=2 * T * C
        ),
    )(tokens, gate_weight, up_weight, hidden_grad)


def shards(tokens, gate_weight, up_weight, hidden_grad, step_index):
    devices = lax.axis_size("dp")
    levels = (devices // 4).bit_length() - 1
    branches = [functools.partial(call_step, level, devices) for level in range(levels)]
    return lax.switch(
        step_index[0] % levels, branches, tokens, gate_weight, up_weight, hidden_grad
    )


def solution(mesh):
    placed = (P("dp", "tensor"), P("dp", "tensor"), P("dp", "tensor"), P("dp", "tensor"), P())
    return jax.shard_map(
        shards,
        mesh=mesh,
        in_specs=placed,
        out_specs=(P("dp", "tensor"), P("dp", "tensor")),
        check_vma=False,
    )
```

```python
import functools

import jax
import jax.numpy as jnp
from jax import lax
from jax.experimental import pallas as pl
from jax.experimental.pallas import tpu as pltpu
from jax.sharding import PartitionSpec as P

MESH = pl.DeviceIdType.MESH
BF16, F32 = jnp.bfloat16, jnp.float32
PARTS = 3

X_Z, X_Y, X_FAR, X_NEAR = 0, 1, 3, 7
W_CORE, COT, X_CORE, PART, DELTA, STEP = 11, 13, 14, 15, 15 + PARTS, 15 + 2 * PARTS
G_NEAR = 15 + 3 * PARTS
G_FAR, G_Y, G_Z, SENDS = G_NEAR + 4, G_NEAR + 8, G_NEAR + 10, G_NEAR + 11
R_X, R_W, R_COT, R_XC, R_PART, R_DELTA, R_STEP = 0, 9, 11, 12, 13, 13 + PARTS, 13 + 2 * PARTS
R_NEAR = 13 + 3 * PARTS
R_FAR, R_Y, R_Z, RECVS = R_NEAR + 4, R_NEAR + 8, R_NEAR + 10, R_NEAR + 11


def step_kernel(
    level, groups_dp, tok, gw, uw, cot, avg_ref, ig_ref,
    xin, xz, xs, xt, wgb, wub, wgt, wut, hg, pf, sb, rb, ud, us, gd, st, pr,
    acc, near_out, near_in, far_out, far_in, y_out, y_in, z_out, z_in,
    ig_buf, snd, rcv, loc,
):
    F, T = tok.shape
    C, R = gw.shape
    n_part = C // PARTS
    dp, t = lax.axis_index("dp"), lax.axis_index("tensor")
    core, side = lax.rem(dp, 2), lax.rem(dp // 2, 2)
    x, zh = t // 2, lax.rem(t, 2)
    place = lax.rem(x - 2 * side + 4, 4)
    home = place < 2
    away = place >= 2
    odd = lax.rem(place, 2)
    prim = jnp.where(home, odd, 1 - odd)
    xbit = lax.rem(x, 2)

    sibling = (dp + 1 - 2 * core, t)
    across = (dp + 2 - 4 * side, t)
    anti = (dp, t + 1 - 2 * zh)
    near = (dp, (x + 1 - 2 * xbit) * 2 + zh)
    far = (dp, lax.rem(2 * side + 3 - place, 4) * 2 + zh)
    shift = 4 * 2**level
    target = (lax.rem(dp + shift, groups_dp), t)
    origin = (lax.rem(dp + groups_dp - shift, groups_dp), t)

    partners = [sibling, across, anti, near, far, target]
    if 2 * shift != groups_dp:
        partners.append(origin)
    barrier = pltpu.get_barrier_semaphore()
    for partner in partners:
        pl.semaphore_signal(barrier, inc=1, device_id=partner, device_id_type=MESH)
    pl.semaphore_wait(barrier, len(partners))

    drain = []

    def remote(src, dst, s, r, device):
        return pltpu.make_async_remote_copy(
            src_ref=src, dst_ref=dst, send_sem=snd.at[s], recv_sem=rcv.at[r],
            device_id=device, device_id_type=MESH,
        )

    def rows_of(r, size):
        return pl.ds(pl.multiple_of(r * size, size), size)

    def block_of(ref, i, z, y):
        return ref.at[i, rows_of(z, F), rows_of(y, T)]

    def slot(i, z, y):
        return (i * 2 + z) * 2 + y

    blocks = [(zh, side), (zh, 1 - side), (1 - zh, side), (1 - zh, 1 - side)]

    def to_x(n, src, which, device):
        where = (prim, *blocks[n])
        src = block_of(xin, *where) if src is None else src
        return remote(src, block_of(xin, *where), which + n, R_X + slot(*where), device)

    def x_arrived(i, n):
        where = (i, *blocks[n])
        remote(tok, block_of(xin, *where), X_Z, R_X + slot(*where), anti).wait_recv()

    mine = (xbit, zh, side)
    later = (xbit, 1 - zh, side)
    z_home = remote(tok, block_of(xin, *mine), X_Z, R_X + slot(*mine), anti)
    z_away = remote(tok, xz, X_Z, R_X + 8, anti)
    y_own = remote(tok, block_of(xin, *mine), X_Y, R_X + slot(*mine), across)
    y_anti = remote(xz, block_of(xin, *later), X_Y + 1, R_X + slot(*later), across)
    own_x = pltpu.make_async_copy(tok, block_of(xin, *mine), loc.at[0])
    cot_copy = remote(cot, hg.at[:, rows_of(side, T)], COT, R_COT, across)

    @pl.when(home)
    def _():
        z_home.start()
        to_x(0, tok, X_FAR, far).start()
        to_x(0, tok, X_NEAR, near).start()
        own_x.start()
        cot_copy.start()

    @pl.when(away)
    def _():
        z_away.start()
        y_own.start()

    w_copies = [
        remote(gw, wgb.at[core], W_CORE, R_W, sibling),
        remote(uw, wub.at[core], W_CORE + 1, R_W + 1, sibling),
    ]
    own_copies = [
        pltpu.make_async_copy(gw, wgb.at[core], loc.at[1]),
        pltpu.make_async_copy(uw, wub.at[core], loc.at[2]),
        pltpu.make_async_copy(cot, hg.at[:, rows_of(side, T)], loc.at[3]),
    ]
    for copy in own_copies + w_copies:
        copy.start()

    @pl.when(home)
    def _():
        for n in (1, 2, 3):
            x_arrived(prim, n)
            to_x(n, None, X_FAR, far).start()
            to_x(n, None, X_NEAR, near).start()
        own_x.wait()

    @pl.when(away)
    def _():
        for n in range(4):
            if n == 1:
                z_away.wait_recv()
                y_anti.start()
                cot_copy.start()
            x_arrived(prim, n)
            to_x(n, None, X_FAR, near).start()

    for copy in own_copies:
        copy.wait()
    for copy in w_copies:
        copy.wait_recv()
    for n in range(4):
        x_arrived(1 - prim, n)

    def x_left():
        z_home.wait_send()
        cot_copy.wait_send()
        for copy in w_copies:
            copy.wait_send()
        for n in range(4):
            to_x(n, tok, X_FAR, far).wait_send()

        @pl.when(home)
        def _():
            for n in range(4):
                to_x(n, tok, X_NEAR, near).wait_send()

        @pl.when(away)
        def _():
            y_own.wait_send()
            y_anti.wait_send()

    drain.append(x_left)

    x_copy = remote(xin.at[1 - core], xs, X_CORE, R_XC, sibling)
    x_copy.start()
    drain.append(lambda: x_copy.wait_send())

    def sums_copy(j):
        return remote(sb.at[j], rb.at[j], PART + j, R_PART + j, across)

    def delta_copy(j):
        return remote(ud.at[j], us.at[j], DELTA + j, R_DELTA + j, sibling)

    def step_copy(j):
        return remote(st.at[rows_of(j, n_part)], pr.at[rows_of(j, n_part)], STEP + j, R_STEP + j, target)

    def parts_left(which):
        @pl.loop(0, PARTS)
        def _(j):
            which(j).wait_send()

    @pl.loop(0, PARTS)
    def _(j):
        rows = rows_of(j, n_part)
        for n, w in ((0, wgb), (1, wub)):
            total = jnp.dot(w[0, rows, :], xin[0], preferred_element_type=F32) + jnp.dot(
                w[1, rows, :], xin[1], preferred_element_type=F32
            )
            pf[j, n] = total
            sb[j, n] = total.astype(BF16)
        sums_copy(j).start()

    drain.append(lambda: parts_left(sums_copy))

    @pl.loop(0, PARTS)
    def _(j):
        rows = rows_of(j, n_part)
        for i in range(2):
            wgt[j, i] = wgb[i, rows, :].T
            wut[j, i] = wub[i, rows, :].T

    acc[...] = jnp.zeros_like(acc)
    xt[: 2 * T, :] = xin[core].T
    x_copy.wait_recv()
    xt[2 * T :, :] = xs[...].T
    cot_copy.wait_recv()

    @pl.loop(0, PARTS)
    def _(j):
        sums_copy(j).wait_recv()
        tile = 32 if n_part % 32 == 0 else 16

        @pl.loop(0, n_part // tile)
        def _(r):
            rows = rows_of(r, tile)
            gate = pf[j, 0, rows, :] + rb[j, 0, rows, :].astype(F32)
            up = pf[j, 1, rows, :] + rb[j, 1, rows, :].astype(F32)
            sig = 1.0 / (1.0 + jnp.exp(-gate))
            at = pl.ds(pl.multiple_of(j * n_part + r * tile, tile), tile)
            wide = hg[at, :].astype(F32)
            ud[j, rows, :] = (wide * gate * sig).astype(BF16)
            gd[j, rows, :] = (wide * up * sig * (1.0 + gate * (1.0 - sig))).astype(BF16)

        delta_copy(j).start()

        for i in range(2):
            @pl.loop(0, 2)
            def _(r):
                rows = rows_of(r, R // 2)
                acc[i, rows, :] += jnp.dot(
                    wut[j, i, rows, :], ud[j], preferred_element_type=F32
                ) + jnp.dot(wgt[j, i, rows, :], gd[j], preferred_element_type=F32)

        delta_copy(j).wait_recv()
        grad = jnp.dot(ud[j], xt[: 2 * T, :], preferred_element_type=F32) + jnp.dot(
            us[j], xt[2 * T :, :], preferred_element_type=F32
        )
        rows = rows_of(j, n_part)
        st[rows, :] = (wub[core, rows, :].astype(F32) - 0.002 * grad).astype(BF16)
        step_copy(j).start()

    drain.append(lambda: parts_left(delta_copy))
    drain.append(lambda: parts_left(step_copy))

    pieces = [(1 - zh, 1 - side), (zh, 1 - side), (1 - zh, side), (zh, side)]

    def piece(i, n):
        return block_of(acc, i, *pieces[n])

    def g_near(n):
        return remote(near_out.at[n], near_in.at[n], G_NEAR + n, R_NEAR + n, near)

    def g_far(n):
        return remote(far_out.at[n], far_in.at[n], G_FAR + n, R_FAR + n, far)

    def g_y(n):
        return remote(y_out.at[n], y_in.at[n], G_Y + n, R_Y + n, across)

    def g_z(src):
        return remote(src, z_in, G_Z, R_Z, anti)

    for n in range(4):
        near_out[n] = piece(1 - prim, n)[...].astype(BF16)
        g_near(n).start()

    @pl.when(away)
    def _():
        for n in range(4):
            g_near(n).wait_recv()
            far_out[n] = (piece(prim, n)[...] + near_in[n].astype(F32)).astype(BF16)
            g_far(n).start()
        g_y(0).wait_recv()
        g_z(y_in.at[0]).start()
        g_y(1).wait_recv()
        g_z(z_out).wait_recv()
        ig_buf[...] = (y_in[1].astype(F32) + z_in[...].astype(F32)).astype(BF16)

    @pl.when(home)
    def _():
        def total(n):
            g_near(n).wait_recv()
            g_far(n).wait_recv()
            return piece(prim, n)[...] + near_in[n].astype(F32) + far_in[n].astype(F32)

        for n in range(2):
            y_out[n] = total(n).astype(BF16)
            g_y(n).start()
        z_out[...] = total(2).astype(BF16)
        g_z(z_out).start()
        last = total(3)
        g_z(z_out).wait_recv()
        ig_buf[...] = (last + z_in[...].astype(F32)).astype(BF16)

    ig_copy = pltpu.make_async_copy(ig_buf, ig_ref, loc.at[4])
    ig_copy.start()

    def ig_left():
        ig_copy.wait()
        for n in range(4):
            g_near(n).wait_send()
        g_z(z_out).wait_send()

        @pl.when(home)
        def _():
            for n in range(2):
                g_y(n).wait_send()

        @pl.when(away)
        def _():
            for n in range(4):
                g_far(n).wait_send()

    drain.append(ig_left)

    @pl.loop(0, PARTS)
    def _(j):
        rows = rows_of(j, n_part)
        step_copy(j).wait_recv()
        step_copy(j).wait_send()
        st[rows, :] = (
            (st[rows, :].astype(F32) + pr[rows, :].astype(F32)) * 0.5
        ).astype(BF16)
        pltpu.make_async_copy(st.at[rows], avg_ref.at[rows], loc.at[5 + j]).start()

    drain.pop(-2)

    @pl.loop(0, PARTS)
    def _(j):
        rows = rows_of(j, n_part)
        pltpu.make_async_copy(st.at[rows], avg_ref.at[rows], loc.at[5 + j]).wait()

    for left in drain:
        left()


def call_step(level, groups_dp, tokens, gate_weight, up_weight, hidden_grad):
    F, T = tokens.shape
    C, R = gate_weight.shape
    n_part = C // PARTS
    vmem = pltpu.VMEM
    scratch = [
        vmem((2, R, 2 * T), BF16),
        vmem((F, T), BF16),
        vmem((R, 2 * T), BF16),
        vmem((4 * T, R), BF16),
        vmem((2, C, R), BF16),
        vmem((2, C, R), BF16),
        vmem((PARTS, 2, R, n_part), BF16),
        vmem((PARTS, 2, R, n_part), BF16),
        vmem((C, 2 * T), BF16),
        vmem((PARTS, 2, n_part, 2 * T), F32),
        vmem((PARTS, 2, n_part, 2 * T), BF16),
        vmem((PARTS, 2, n_part, 2 * T), BF16),
        vmem((PARTS, n_part, 2 * T), BF16),
        vmem((PARTS, n_part, 2 * T), BF16),
        vmem((PARTS, n_part, 2 * T), BF16),
        vmem((C, R), BF16),
        vmem((C, R), BF16),
        vmem((2, R, 2 * T), F32),
        vmem((4, F, T), BF16),
        vmem((4, F, T), BF16),
        vmem((4, F, T), BF16),
        vmem((4, F, T), BF16),
        vmem((2, F, T), BF16),
        vmem((2, F, T), BF16),
        vmem((F, T), BF16),
        vmem((F, T), BF16),
        vmem((F, T), BF16),
        pltpu.SemaphoreType.DMA((SENDS,)),
        pltpu.SemaphoreType.DMA((RECVS,)),
        pltpu.SemaphoreType.DMA((5 + PARTS,)),
    ]
    return pl.pallas_call(
        functools.partial(step_kernel, level, groups_dp),
        out_shape=(
            jax.ShapeDtypeStruct((C, R), BF16),
            jax.ShapeDtypeStruct((F, T), BF16),
        ),
        in_specs=[pl.BlockSpec(memory_space=pl.ANY)] * 4,
        out_specs=[pl.BlockSpec(memory_space=pl.ANY)] * 2,
        scratch_shapes=scratch,
        compiler_params=pltpu.CompilerParams(
            collective_id=level, has_side_effects=True, vmem_limit_bytes=56 * 2**20
        ),
        cost_estimate=pl.CostEstimate(
            flops=20 * T * 8 * F * C, bytes_accessed=6 * R * C, transcendentals=2 * T * C
        ),
    )(tokens, gate_weight, up_weight, hidden_grad)


def shards(tokens, gate_weight, up_weight, hidden_grad, step_index):
    devices = lax.axis_size("dp")
    levels = (devices // 4).bit_length() - 1
    branches = [functools.partial(call_step, level, devices) for level in range(levels)]
    averaged_up, input_grad = lax.switch(
        step_index[0] % levels, branches, tokens.T, gate_weight.T, up_weight.T, hidden_grad.T
    )
    return averaged_up.T, input_grad.T


def solution(mesh):
    placed = (P("dp", "tensor"), P("dp", "tensor"), P("dp", "tensor"), P("dp", "tensor"), P())
    return jax.shard_map(
        shards,
        mesh=mesh,
        in_specs=placed,
        out_specs=(P("dp", "tensor"), P("dp", "tensor")),
        check_vma=False,
    )
```

```python
import functools

import jax
import jax.numpy as jnp
from jax import lax
from jax.experimental import pallas as pl
from jax.experimental.pallas import tpu as pltpu
from jax.sharding import PartitionSpec as P

MESH = pl.DeviceIdType.MESH
BF16, F32 = jnp.bfloat16, jnp.float32
PARTS = 3

X_Z, X_Y, X_FAR, X_NEAR, W_CORE, COT, X_CORE, PART = 0, 2, 6, 14, 22, 24, 25, 27
DELTA, STEP, G_NEAR = PART + 2 * PARTS, PART + 4 * PARTS, PART + 5 * PARTS
G_FAR, G_Y, G_Z, SENDS = G_NEAR + 8, G_NEAR + 16, G_NEAR + 20, G_NEAR + 22
R_X, R_W, R_COT, R_XC, R_PART = 0, 18, 20, 21, 23
R_DELTA, R_STEP, R_NEAR = R_PART + 2 * PARTS, R_PART + 4 * PARTS, R_PART + 5 * PARTS
R_FAR, R_Y, R_Z, RECVS = R_NEAR + 8, R_NEAR + 16, R_NEAR + 20, R_NEAR + 22


def step_kernel(
    level, groups_dp, tok, gw, uw, cot, avg_ref, ig_ref,
    xin, xz, xs, xt, wgb, wub, wgt, wut, hg, pf, sb, rb, ud, us, gd, st, pr,
    ug, acc, near_out, near_in, far_out, far_in, y_out, y_in, z_out, z_in,
    ig_buf, snd, rcv, loc,
):
    F, T = tok.shape
    C, R = gw.shape
    n_part = C // PARTS
    dp, t = lax.axis_index("dp"), lax.axis_index("tensor")
    core, side = lax.rem(dp, 2), lax.rem(dp // 2, 2)
    x, zh = t // 2, lax.rem(t, 2)
    place = lax.rem(x - 2 * side + 4, 4)
    home = place < 2
    away = place >= 2
    odd = lax.rem(place, 2)
    prim = jnp.where(home, odd, 1 - odd)
    xbit = lax.rem(x, 2)

    sibling = (dp + 1 - 2 * core, t)
    across = (dp + 2 - 4 * side, t)
    anti = (dp, t + 1 - 2 * zh)
    near = (dp, (x + 1 - 2 * xbit) * 2 + zh)
    far = (dp, lax.rem(2 * side + 3 - place, 4) * 2 + zh)
    shift = 4 * 2**level
    target = (lax.rem(dp + shift, groups_dp), t)
    origin = (lax.rem(dp + groups_dp - shift, groups_dp), t)

    partners = [sibling, across, anti, near, far, target]
    if 2 * shift != groups_dp:
        partners.append(origin)
    barrier = pltpu.get_barrier_semaphore()
    for partner in partners:
        pl.semaphore_signal(barrier, inc=1, device_id=partner, device_id_type=MESH)
    pl.semaphore_wait(barrier, len(partners))

    drain = []

    def remote(src, dst, s, r, device):
        return pltpu.make_async_remote_copy(
            src_ref=src, dst_ref=dst, send_sem=snd.at[s], recv_sem=rcv.at[r],
            device_id=device, device_id_type=MESH,
        )

    def rows_of(r, size):
        return pl.ds(pl.multiple_of(r * size, size), size)

    H = F // 2

    def half_of(ref, a):
        return ref.at[rows_of(a, H)]

    def block_of(ref, i, z, y, a):
        return ref.at[i, y, rows_of(z * 2 + a, H)]

    def slot(i, z, y, a):
        return ((i * 2 + z) * 2 + y) * 2 + a

    blocks = [(zh, side), (zh, 1 - side), (1 - zh, side), (1 - zh, 1 - side)]

    def to_x(n, a, which, device):
        where = (prim, *blocks[n], a)
        return remote(block_of(xin, *where), block_of(xin, *where), which + 2 * n + a, R_X + slot(*where), device)

    def own_to_x(a, which, device):
        where = (prim, *blocks[0], a)
        return remote(half_of(tok, a), block_of(xin, *where), which + a, R_X + slot(*where), device)

    def x_arrived(i, n, a):
        where = (i, *blocks[n], a)
        remote(half_of(tok, a), block_of(xin, *where), X_Z, R_X + slot(*where), anti).wait_recv()

    mine = (xbit, zh, side)
    later = (xbit, 1 - zh, side)

    def z_home(a):
        return remote(half_of(tok, a), block_of(xin, *mine, a), X_Z + a, R_X + slot(*mine, a), anti)

    def z_away(a):
        return remote(half_of(tok, a), half_of(xz, a), X_Z + a, R_X + 16 + a, anti)

    def y_own(a):
        return remote(half_of(tok, a), block_of(xin, *mine, a), X_Y + a, R_X + slot(*mine, a), across)

    def y_anti(a):
        return remote(half_of(xz, a), block_of(xin, *later, a), X_Y + 2 + a, R_X + slot(*later, a), across)

    own_x = pltpu.make_async_copy(tok, xin.at[xbit, side, rows_of(zh, F)], loc.at[0])
    cot_copy = remote(cot, hg.at[side], COT, R_COT, across)

    @pl.when(home)
    def _():
        for a in range(2):
            z_home(a).start()
            own_to_x(a, X_FAR, far).start()
            own_to_x(a, X_NEAR, near).start()
        own_x.start()
        cot_copy.start()

    @pl.when(away)
    def _():
        for a in range(2):
            z_away(a).start()
            y_own(a).start()

    w_copies = [
        remote(gw, wgb.at[core], W_CORE, R_W, sibling),
        remote(uw, wub.at[core], W_CORE + 1, R_W + 1, sibling),
    ]
    own_copies = [
        pltpu.make_async_copy(gw, wgb.at[core], loc.at[1]),
        pltpu.make_async_copy(uw, wub.at[core], loc.at[2]),
        pltpu.make_async_copy(cot, hg.at[side], loc.at[3]),
    ]
    for copy in own_copies + w_copies:
        copy.start()

    @pl.when(home)
    def _():
        for n, a in ((1, 0), (2, 0), (1, 1), (2, 1)):
            x_arrived(prim, n, a)
            to_x(n, a, X_FAR, far).start()
            to_x(n, a, X_NEAR, near).start()
        own_x.wait()

    @pl.when(away)
    def _():
        def hand_on(n, a):
            x_arrived(prim, n, a)
            to_x(n, a, X_FAR, near).start()

        hand_on(0, 0)
        hand_on(0, 1)
        cot_copy.start()
        for a in range(2):
            z_away(a).wait_recv()
            y_anti(a).start()
            hand_on(1, a)
            hand_on(2, a)

    def forward_last():
        for a in range(2):
            x_arrived(prim, 3, a)

            @pl.when(home)
            def _():
                to_x(3, a, X_FAR, far).start()
                to_x(3, a, X_NEAR, near).start()

            @pl.when(away)
            def _():
                to_x(3, a, X_FAR, near).start()

    for copy in own_copies:
        copy.wait()
    for copy in w_copies:
        copy.wait_recv()
    for n, a in ((0, 0), (0, 1), (2, 0), (2, 1)):
        x_arrived(1 - prim, n, a)

    def x_left():
        cot_copy.wait_send()
        for copy in w_copies:
            copy.wait_send()
        for a in range(2):
            z_home(a).wait_send()
            for n in range(4):
                to_x(n, a, X_FAR, far).wait_send()

        @pl.when(home)
        def _():
            for a in range(2):
                for n in range(4):
                    to_x(n, a, X_NEAR, near).wait_send()

        @pl.when(away)
        def _():
            for a in range(2):
                y_own(a).wait_send()
                y_anti(a).wait_send()

    drain.append(x_left)

    half_y = (1 - side, side)

    def x_copy(y, n):
        return remote(xin.at[1 - core, y], xs.at[y], X_CORE + n, R_XC + n, sibling)

    def sums_copy(h, j):
        return remote(sb.at[h, j], rb.at[h, j], PART + h * PARTS + j, R_PART + h * PARTS + j, across)

    def delta_copy(h, j):
        rows = rows_of(j, n_part)
        at = h * PARTS + j
        return remote(ud.at[h, rows], us.at[h, rows], DELTA + at, R_DELTA + at, sibling)

    def step_copy(j):
        return remote(st.at[rows_of(j, n_part)], pr.at[rows_of(j, n_part)], STEP + j, R_STEP + j, target)

    def sums(h, j):
        rows, y = rows_of(j, n_part), half_y[1 - h]
        for n, w in ((0, wgb), (1, wub)):
            total = jnp.dot(w[0, rows, :], xin[0, y], preferred_element_type=F32) + jnp.dot(
                w[1, rows, :], xin[1, y], preferred_element_type=F32
            )
            pf[h, j, n] = total
            sb[h, j, n] = total.astype(BF16)

    by_parts = level == 3
    order = [(h, j) for h in range(2) for j in range(PARTS)]
    if by_parts:
        order = [(h, j) for j in range(PARTS) for h in range(2)]
    flight = 2 if by_parts else len(order)

    def next_sums(q):
        sums_copy(*order[q]).wait_send()
        if q + flight < len(order):
            sums_copy(*order[q + flight]).start()

    sums(0, 0)
    sums_copy(0, 0).start()
    forward_last()
    x_copy(side, 0).start()

    @pl.loop(1, PARTS)
    def _(j):
        sums(0, j)

    started = 1
    while started < flight and order[started][0] == 0:
        sums_copy(*order[started]).start()
        started += 1

    for n, a in ((1, 0), (1, 1), (3, 0), (3, 1)):
        x_arrived(1 - prim, n, a)
    x_copy(1 - side, 1).start()

    @pl.loop(0, PARTS)
    def _(j):
        sums(1, j)

    for q in range(started, flight):
        sums_copy(*order[q]).start()

    def sums_left():
        x_copy(side, 0).wait_send()
        x_copy(1 - side, 1).wait_send()
        for h in range(2):
            @pl.loop(0, PARTS)
            def _(j):
                delta_copy(h, j).wait_send()

    drain.append(sums_left)

    for n, y in ((0, side), (1, 1 - side)):
        xt[1 - n, 0] = xin[core, y].T
        x_copy(y, n).wait_recv()
        xt[1 - n, 1] = xs[y].T
    cot_copy.wait_recv()

    def deltas(h, j):
        y = half_y[h]
        part = rows_of(j, n_part)
        if h == 0:
            for i in range(2):
                wgt[j, i] = wgb[i, part, :].T
                wut[j, i] = wub[i, part, :].T
        next_sums(order.index((h, j)))
        sums_copy(h, j).wait_recv()
        tile = 32 if n_part % 32 == 0 else 16

        @pl.loop(0, n_part // tile)
        def _(r):
            rows = rows_of(r, tile)
            at = pl.ds(pl.multiple_of(j * n_part + r * tile, tile), tile)
            gate = pf[1 - h, j, 0, rows, :] + rb[h, j, 0, rows, :].astype(F32)
            up = pf[1 - h, j, 1, rows, :] + rb[h, j, 1, rows, :].astype(F32)
            sig = 1.0 / (1.0 + jnp.exp(-gate))
            wide = hg[y, at, :].astype(F32)
            ud[h, at, :] = (wide * gate * sig).astype(BF16)
            gd[at, :] = (wide * up * sig * (1.0 + gate * (1.0 - sig))).astype(BF16)

        delta_copy(h, j).start()
        for i in range(2):
            new = jnp.dot(wut[j, i], ud[h, part, :], preferred_element_type=F32) + jnp.dot(
                wgt[j, i], gd[part, :], preferred_element_type=F32
            )
            if j == 0:
                acc[i, y] = new
            else:
                acc[i, y] += new
        delta_copy(h, j).wait_recv()
        grad = jnp.dot(ud[h, part, :], xt[h, 0], preferred_element_type=F32) + jnp.dot(
            us[h, part, :], xt[h, 1], preferred_element_type=F32
        )
        if h == 0:
            ug[part, :] = grad
        else:
            grad += ug[part, :]
            st[part, :] = (wub[core, part, :].astype(F32) - 0.002 * grad).astype(BF16)
            step_copy(j).start()

    pieces = [(1 - zh, 1 - side), (zh, 1 - side), (1 - zh, side), (zh, side)]

    def piece(i, n, a):
        return block_of(acc, i, *pieces[n], a)

    def g_near(n, a):
        m = 2 * n + a
        return remote(near_out.at[m], near_in.at[m], G_NEAR + m, R_NEAR + m, near)

    def g_far(n, a):
        m = 2 * n + a
        return remote(far_out.at[m], far_in.at[m], G_FAR + m, R_FAR + m, far)

    def g_y(n, a):
        m = 2 * n + a
        return remote(y_out.at[m], y_in.at[m], G_Y + m, R_Y + m, across)

    def g_z(src, a):
        return remote(src, z_in.at[a], G_Z + a, R_Z + a, anti)

    both = [(n, a) for n in range(2) for a in range(2)]

    def nearby(first):
        for n, a in both:
            n = n + first
            near_out[2 * n + a] = piece(1 - prim, n, a)[...].astype(BF16)
            g_near(n, a).start()

    def relay(first):
        @pl.when(away)
        def _():
            for n, a in both:
                n = n + first
                m = 2 * n + a
                g_near(n, a).wait_recv()
                far_out[m] = (piece(prim, n, a)[...] + near_in[m].astype(F32)).astype(BF16)
                g_far(n, a).start()

    def total(n, a):
        g_near(n, a).wait_recv()
        g_far(n, a).wait_recv()
        m = 2 * n + a
        return piece(prim, n, a)[...] + near_in[m].astype(F32) + far_in[m].astype(F32)

    def to_across():
        @pl.when(home)
        def _():
            for n, a in both:
                y_out[2 * n + a] = total(n, a).astype(BF16)
                g_y(n, a).start()

    then = {(0, PARTS - 1): [lambda: nearby(0)]}
    if not by_parts:
        then[1, 0] = [lambda: relay(0)]
        then[1, PARTS - 2] = [to_across]
    else:
        then[1, PARTS - 1] = [lambda: nearby(2), lambda: relay(0), to_across]
    for h, j in order:
        deltas(h, j)
        for step in then.get((h, j), []):
            step()

    if not by_parts:
        nearby(2)
    relay(2)

    @pl.when(away)
    def _():
        for a in range(2):
            g_y(0, a).wait_recv()
            g_z(y_in.at[a], a).start()
        for a in range(2):
            g_y(1, a).wait_recv()
            g_z(z_out.at[a], a).wait_recv()
            ig_buf[rows_of(a, H), :] = (y_in[2 + a].astype(F32) + z_in[a].astype(F32)).astype(BF16)

    @pl.when(home)
    def _():
        for a in range(2):
            z_out[a] = total(2, a).astype(BF16)
            g_z(z_out.at[a], a).start()
        for a in range(2):
            last = total(3, a)
            g_z(z_out.at[a], a).wait_recv()
            ig_buf[rows_of(a, H), :] = (last + z_in[a].astype(F32)).astype(BF16)

    ig_copy = pltpu.make_async_copy(ig_buf, ig_ref, loc.at[4])
    ig_copy.start()

    def ig_left():
        ig_copy.wait()
        for a in range(2):
            for n in range(4):
                g_near(n, a).wait_send()
            g_z(z_out.at[a], a).wait_send()

        @pl.when(home)
        def _():
            for n, a in both:
                g_y(n, a).wait_send()

        @pl.when(away)
        def _():
            for a in range(2):
                for n in range(4):
                    g_far(n, a).wait_send()

    drain.append(ig_left)

    @pl.loop(0, PARTS)
    def _(j):
        rows = rows_of(j, n_part)
        step_copy(j).wait_recv()
        step_copy(j).wait_send()
        st[rows, :] = (
            (st[rows, :].astype(F32) + pr[rows, :].astype(F32)) * 0.5
        ).astype(BF16)
        pltpu.make_async_copy(st.at[rows], avg_ref.at[rows], loc.at[5 + j]).start()

    @pl.loop(0, PARTS)
    def _(j):
        rows = rows_of(j, n_part)
        pltpu.make_async_copy(st.at[rows], avg_ref.at[rows], loc.at[5 + j]).wait()

    for left in drain:
        left()


def call_step(level, groups_dp, tokens, gate_weight, up_weight, hidden_grad):
    F, T = tokens.shape
    C, R = gate_weight.shape
    n_part = C // PARTS
    vmem = pltpu.VMEM
    scratch = [
        vmem((2, 2, R, T), BF16),
        vmem((F, T), BF16),
        vmem((2, R, T), BF16),
        vmem((2, 2, T, R), BF16),
        vmem((2, C, R), BF16),
        vmem((2, C, R), BF16),
        vmem((PARTS, 2, R, n_part), BF16),
        vmem((PARTS, 2, R, n_part), BF16),
        vmem((2, C, T), BF16),
        vmem((2, PARTS, 2, n_part, T), F32),
        vmem((2, PARTS, 2, n_part, T), BF16),
        vmem((2, PARTS, 2, n_part, T), BF16),
        vmem((2, C, T), BF16),
        vmem((2, C, T), BF16),
        vmem((C, T), BF16),
        vmem((C, R), BF16),
        vmem((C, R), BF16),
        vmem((C, R), F32),
        vmem((2, 2, R, T), F32),
        vmem((8, F // 2, T), BF16),
        vmem((8, F // 2, T), BF16),
        vmem((8, F // 2, T), BF16),
        vmem((8, F // 2, T), BF16),
        vmem((4, F // 2, T), BF16),
        vmem((4, F // 2, T), BF16),
        vmem((2, F // 2, T), BF16),
        vmem((2, F // 2, T), BF16),
        vmem((F, T), BF16),
        pltpu.SemaphoreType.DMA((SENDS,)),
        pltpu.SemaphoreType.DMA((RECVS,)),
        pltpu.SemaphoreType.DMA((5 + PARTS,)),
    ]
    return pl.pallas_call(
        functools.partial(step_kernel, level, groups_dp),
        out_shape=(
            jax.ShapeDtypeStruct((C, R), BF16),
            jax.ShapeDtypeStruct((F, T), BF16),
        ),
        in_specs=[pl.BlockSpec(memory_space=pl.ANY)] * 4,
        out_specs=[pl.BlockSpec(memory_space=pl.ANY)] * 2,
        scratch_shapes=scratch,
        compiler_params=pltpu.CompilerParams(
            collective_id=level, has_side_effects=True, vmem_limit_bytes=56 * 2**20
        ),
        cost_estimate=pl.CostEstimate(
            flops=20 * T * 8 * F * C, bytes_accessed=6 * R * C, transcendentals=2 * T * C
        ),
    )(tokens, gate_weight, up_weight, hidden_grad)


def shards(tokens, gate_weight, up_weight, hidden_grad, step_index):
    devices = lax.axis_size("dp")
    levels = (devices // 4).bit_length() - 1
    branches = [functools.partial(call_step, level, devices) for level in range(levels)]
    averaged_up, input_grad = lax.switch(
        step_index[0] % levels, branches, tokens.T, gate_weight.T, up_weight.T, hidden_grad.T
    )
    return averaged_up.T, input_grad.T


def solution(mesh):
    placed = (P("dp", "tensor"), P("dp", "tensor"), P("dp", "tensor"), P("dp", "tensor"), P())
    return jax.shard_map(
        shards,
        mesh=mesh,
        in_specs=placed,
        out_specs=(P("dp", "tensor"), P("dp", "tensor")),
        check_vma=False,
    )
```

```python
import functools

import jax
import jax.numpy as jnp
from jax import lax
from jax.experimental import pallas as pl
from jax.experimental.pallas import tpu as pltpu
from jax.sharding import PartitionSpec as P

MESH = pl.DeviceIdType.MESH
BF16, F32 = jnp.bfloat16, jnp.float32
PARTS = 3

X_Z, X_Y, X_FAR, X_NEAR, W_CORE, COT, X_CORE, PART = 0, 2, 6, 14, 22, 24, 25, 27
DELTA, STEP, G_NEAR = PART + 3 * PARTS, PART + 5 * PARTS, PART + 6 * PARTS
G_FAR, G_Y, G_Z, SENDS = G_NEAR + 8, G_NEAR + 16, G_NEAR + 20, G_NEAR + 22
R_X, R_W, R_COT, R_XC, R_PART = 0, 18, 20, 21, 23
R_DELTA, R_STEP, R_NEAR = R_PART + 3 * PARTS, R_PART + 5 * PARTS, R_PART + 6 * PARTS
R_FAR, R_Y, R_Z, RECVS = R_NEAR + 8, R_NEAR + 16, R_NEAR + 20, R_NEAR + 22


def step_kernel(
    level, groups_dp, tok, gw, uw, cot, avg_ref, ig_ref,
    xin, xz, xs, xt, wgb, wub, wgt, wut, hg, pf, sb, rb, ud, us, gd, st, pr,
    ug, acc, near_out, near_in, far_out, far_in, y_out, y_in, z_out, z_in,
    ig_buf, snd, rcv, loc,
):
    F, T = tok.shape
    C, R = gw.shape
    n_part = C // PARTS
    dp, t = lax.axis_index("dp"), lax.axis_index("tensor")
    core, side = lax.rem(dp, 2), lax.rem(dp // 2, 2)
    x, zh = t // 2, lax.rem(t, 2)
    place = lax.rem(x - 2 * side + 4, 4)
    home = place < 2
    away = place >= 2
    odd = lax.rem(place, 2)
    prim = jnp.where(home, odd, 1 - odd)
    xbit = lax.rem(x, 2)

    sibling = (dp + 1 - 2 * core, t)
    across = (dp + 2 - 4 * side, t)
    anti = (dp, t + 1 - 2 * zh)
    near = (dp, (x + 1 - 2 * xbit) * 2 + zh)
    far = (dp, lax.rem(2 * side + 3 - place, 4) * 2 + zh)
    shift = 4 * 2**level
    target = (lax.rem(dp + shift, groups_dp), t)
    origin = (lax.rem(dp + groups_dp - shift, groups_dp), t)

    partners = [sibling, across, anti, near, far, target]
    if 2 * shift != groups_dp:
        partners.append(origin)
    barrier = pltpu.get_barrier_semaphore()
    for partner in partners:
        pl.semaphore_signal(barrier, inc=1, device_id=partner, device_id_type=MESH)
    pl.semaphore_wait(barrier, len(partners))

    drain = []

    def remote(src, dst, s, r, device):
        return pltpu.make_async_remote_copy(
            src_ref=src, dst_ref=dst, send_sem=snd.at[s], recv_sem=rcv.at[r],
            device_id=device, device_id_type=MESH,
        )

    def rows_of(r, size):
        return pl.ds(pl.multiple_of(r * size, size), size)

    H, Q = F // 2, T // 2

    def half_of(ref, a):
        return ref.at[:, a * Q : (a + 1) * Q]

    def block_of(ref, i, z, y, a):
        return ref.at[i, y, rows_of(z, F), a * Q : (a + 1) * Q]

    def slot(i, z, y, a):
        return ((i * 2 + z) * 2 + y) * 2 + a

    blocks = [(zh, side), (zh, 1 - side), (1 - zh, side), (1 - zh, 1 - side)]

    def to_x(n, a, which, device):
        where = (prim, *blocks[n], a)
        return remote(block_of(xin, *where), block_of(xin, *where), which + 2 * n + a, R_X + slot(*where), device)

    def own_to_x(a, which, device):
        where = (prim, *blocks[0], a)
        return remote(half_of(tok, a), block_of(xin, *where), which + a, R_X + slot(*where), device)

    def x_arrived(i, n, a):
        where = (i, *blocks[n], a)
        remote(half_of(tok, a), block_of(xin, *where), X_Z, R_X + slot(*where), anti).wait_recv()

    mine = (xbit, zh, side)
    later = (xbit, 1 - zh, side)

    def z_home(a):
        return remote(half_of(tok, a), block_of(xin, *mine, a), X_Z + a, R_X + slot(*mine, a), anti)

    def z_away(a):
        return remote(half_of(tok, a), half_of(xz, a), X_Z + a, R_X + 16 + a, anti)

    def y_own(a):
        return remote(half_of(tok, a), block_of(xin, *mine, a), X_Y + a, R_X + slot(*mine, a), across)

    def y_anti(a):
        return remote(half_of(xz, a), block_of(xin, *later, a), X_Y + 2 + a, R_X + slot(*later, a), across)

    own_x = pltpu.make_async_copy(tok, xin.at[xbit, side, rows_of(zh, F)], loc.at[0])
    cot_copy = remote(cot, hg.at[side], COT, R_COT, across)

    @pl.when(home)
    def _():
        for a in range(2):
            z_home(a).start()
            own_to_x(a, X_FAR, far).start()
            own_to_x(a, X_NEAR, near).start()
        own_x.start()
        cot_copy.start()

    @pl.when(away)
    def _():
        for a in range(2):
            z_away(a).start()
            y_own(a).start()

    w_copies = [
        remote(gw, wgb.at[core], W_CORE, R_W, sibling),
        remote(uw, wub.at[core], W_CORE + 1, R_W + 1, sibling),
    ]
    own_copies = [
        pltpu.make_async_copy(gw, wgb.at[core], loc.at[1]),
        pltpu.make_async_copy(uw, wub.at[core], loc.at[2]),
        pltpu.make_async_copy(cot, hg.at[side], loc.at[3]),
    ]
    for copy in own_copies + w_copies:
        copy.start()

    @pl.when(home)
    def _():
        for n, a in ((1, 0), (2, 0), (1, 1), (2, 1)):
            x_arrived(prim, n, a)
            to_x(n, a, X_FAR, far).start()
            to_x(n, a, X_NEAR, near).start()
        own_x.wait()

    @pl.when(away)
    def _():
        def hand_on(n, a):
            x_arrived(prim, n, a)
            to_x(n, a, X_FAR, near).start()

        hand_on(0, 0)
        hand_on(0, 1)
        cot_copy.start()
        for a in range(2):
            z_away(a).wait_recv()
            y_anti(a).start()
            hand_on(1, a)
            hand_on(2, a)

    def forward_last():
        for a in range(2):
            x_arrived(prim, 3, a)

            @pl.when(home)
            def _():
                to_x(3, a, X_FAR, far).start()
                to_x(3, a, X_NEAR, near).start()

            @pl.when(away)
            def _():
                to_x(3, a, X_FAR, near).start()

    for copy in own_copies:
        copy.wait()
    for copy in w_copies:
        copy.wait_recv()
    def x_left():
        cot_copy.wait_send()
        for copy in w_copies:
            copy.wait_send()
        for a in range(2):
            z_home(a).wait_send()
            for n in range(4):
                to_x(n, a, X_FAR, far).wait_send()

        @pl.when(home)
        def _():
            for a in range(2):
                for n in range(4):
                    to_x(n, a, X_NEAR, near).wait_send()

        @pl.when(away)
        def _():
            for a in range(2):
                y_own(a).wait_send()
                y_anti(a).wait_send()

    drain.append(x_left)

    half_y = (1 - side, side)

    def x_copy(y, n):
        return remote(xin.at[1 - core, y], xs.at[y], X_CORE + n, R_XC + n, sibling)

    def sums_copy(h, j, a):
        at = (2 * h + a) * PARTS + j
        columns = slice(a * Q, (a + 1) * Q) if h == 0 else slice(None)
        view = (h, j, slice(None), slice(None), columns)
        return remote(sb.at[view], rb.at[view], PART + at, R_PART + at, across)

    def halves(h):
        return (0, 1) if h == 0 else (0,)

    def delta_copy(h, j):
        rows = rows_of(j, n_part)
        at = h * PARTS + j
        return remote(ud.at[h, rows], us.at[h, rows], DELTA + at, R_DELTA + at, sibling)

    def step_copy(j):
        return remote(st.at[rows_of(j, n_part)], pr.at[rows_of(j, n_part)], STEP + j, R_STEP + j, target)

    def sums(h, j, a):
        rows, y = rows_of(j, n_part), half_y[1 - h]
        columns = slice(a * Q, (a + 1) * Q) if h == 0 else slice(None)
        for n, w in ((0, wgb), (1, wub)):
            total = jnp.dot(
                w[0, rows, :], xin[0, y, :, columns], preferred_element_type=F32
            ) + jnp.dot(w[1, rows, :], xin[1, y, :, columns], preferred_element_type=F32)
            pf[h, j, n, :, columns] = total
            sb[h, j, n, :, columns] = total.astype(BF16)

    by_parts = level == 3
    order = [(h, j) for h in range(2) for j in range(PARTS)]
    if by_parts:
        order = [(h, j) for j in range(PARTS) for h in range(2)]
    flight = 2 if by_parts else len(order)

    def start_sums(q):
        h, j = order[q]
        for a in halves(h):
            sums_copy(h, j, a).start()

    def next_sums(q):
        h, j = order[q]
        for a in halves(h):
            sums_copy(h, j, a).wait_send()
        if q + flight < len(order):
            start_sums(q + flight)

    for a in range(2):
        x_arrived(1 - prim, 0, a)
        x_arrived(1 - prim, 2, a)

        @pl.loop(0, PARTS)
        def _(j):
            sums(0, j, a)
            if not by_parts:
                sums_copy(0, j, a).start()

        if by_parts:
            sums_copy(0, 0, a).start()
        if a == 0:
            forward_last()
    x_copy(side, 0).start()
    for n, a in ((1, 0), (1, 1), (3, 0), (3, 1)):
        x_arrived(1 - prim, n, a)
    x_copy(1 - side, 1).start()

    @pl.loop(0, PARTS)
    def _(j):
        sums(1, j, 0)
        if not by_parts:
            sums_copy(1, j, 0).start()

    if by_parts:
        start_sums(1)

    def sums_left():
        x_copy(side, 0).wait_send()
        x_copy(1 - side, 1).wait_send()
        for h in range(2):
            @pl.loop(0, PARTS)
            def _(j):
                delta_copy(h, j).wait_send()

    drain.append(sums_left)

    for n, y in ((0, side), (1, 1 - side)):
        xt[1 - n, 0] = xin[core, y].T
        x_copy(y, n).wait_recv()
        xt[1 - n, 1] = xs[y].T
    cot_copy.wait_recv()

    def deltas(h, j):
        y = half_y[h]
        part = rows_of(j, n_part)
        if h == 0:
            for i in range(2):
                wgt[j, i] = wgb[i, part, :].T
                wut[j, i] = wub[i, part, :].T
        next_sums(order.index((h, j)))
        for a in halves(h):
            sums_copy(h, j, a).wait_recv()
        tile = 32 if n_part % 32 == 0 else 16

        @pl.loop(0, n_part // tile)
        def _(r):
            rows = rows_of(r, tile)
            at = pl.ds(pl.multiple_of(j * n_part + r * tile, tile), tile)
            gate = pf[1 - h, j, 0, rows, :] + rb[h, j, 0, rows, :].astype(F32)
            up = pf[1 - h, j, 1, rows, :] + rb[h, j, 1, rows, :].astype(F32)
            sig = 1.0 / (1.0 + jnp.exp(-gate))
            wide = hg[y, at, :].astype(F32)
            ud[h, at, :] = (wide * gate * sig).astype(BF16)
            gd[at, :] = (wide * up * sig * (1.0 + gate * (1.0 - sig))).astype(BF16)

        delta_copy(h, j).start()
        for i in range(2):
            new = jnp.dot(wut[j, i], ud[h, part, :], preferred_element_type=F32) + jnp.dot(
                wgt[j, i], gd[part, :], preferred_element_type=F32
            )
            if j == 0:
                acc[i, y] = new
            else:
                acc[i, y] += new
        delta_copy(h, j).wait_recv()
        grad = jnp.dot(ud[h, part, :], xt[h, 0], preferred_element_type=F32) + jnp.dot(
            us[h, part, :], xt[h, 1], preferred_element_type=F32
        )
        if h == 0:
            ug[part, :] = grad
        else:
            grad += ug[part, :]
            st[part, :] = (wub[core, part, :].astype(F32) - 0.002 * grad).astype(BF16)
            step_copy(j).start()

    pieces = [(1 - zh, 1 - side), (zh, 1 - side), (1 - zh, side), (zh, side)]

    def piece(i, n, a):
        z, y = pieces[n]
        return acc.at[i, y, rows_of(z * 2 + a, H)]

    def g_near(n, a):
        m = 2 * n + a
        return remote(near_out.at[m], near_in.at[m], G_NEAR + m, R_NEAR + m, near)

    def g_far(n, a):
        m = 2 * n + a
        return remote(far_out.at[m], far_in.at[m], G_FAR + m, R_FAR + m, far)

    def g_y(n, a):
        m = 2 * n + a
        return remote(y_out.at[m], y_in.at[m], G_Y + m, R_Y + m, across)

    def g_z(src, a):
        return remote(src, z_in.at[a], G_Z + a, R_Z + a, anti)

    both = [(n, a) for n in range(2) for a in range(2)]

    def nearby(first):
        for n, a in both:
            n = n + first
            near_out[2 * n + a] = piece(1 - prim, n, a)[...].astype(BF16)
            g_near(n, a).start()

    def relay(first):
        @pl.when(away)
        def _():
            for n, a in both:
                n = n + first
                m = 2 * n + a
                g_near(n, a).wait_recv()
                far_out[m] = (piece(prim, n, a)[...] + near_in[m].astype(F32)).astype(BF16)
                g_far(n, a).start()

    def total(n, a):
        g_near(n, a).wait_recv()
        g_far(n, a).wait_recv()
        m = 2 * n + a
        return piece(prim, n, a)[...] + near_in[m].astype(F32) + far_in[m].astype(F32)

    def to_across():
        @pl.when(home)
        def _():
            for n, a in both:
                y_out[2 * n + a] = total(n, a).astype(BF16)
                g_y(n, a).start()

    then = {(0, PARTS - 1): [lambda: nearby(0)]}
    if not by_parts:
        then[1, 0] = [lambda: relay(0)]
        then[1, PARTS - 2] = [to_across]
    else:
        then[1, PARTS - 1] = [lambda: nearby(2), lambda: relay(0), to_across]
    for h, j in order:
        deltas(h, j)
        for step in then.get((h, j), []):
            step()

    if not by_parts:
        nearby(2)
    relay(2)

    @pl.when(away)
    def _():
        for a in range(2):
            g_y(0, a).wait_recv()
            g_z(y_in.at[a], a).start()
        for a in range(2):
            g_y(1, a).wait_recv()
            g_z(z_out.at[a], a).wait_recv()
            ig_buf[rows_of(a, H), :] = (y_in[2 + a].astype(F32) + z_in[a].astype(F32)).astype(BF16)

    @pl.when(home)
    def _():
        for a in range(2):
            z_out[a] = total(2, a).astype(BF16)
            g_z(z_out.at[a], a).start()
        for a in range(2):
            last = total(3, a)
            g_z(z_out.at[a], a).wait_recv()
            ig_buf[rows_of(a, H), :] = (last + z_in[a].astype(F32)).astype(BF16)

    ig_copy = pltpu.make_async_copy(ig_buf, ig_ref, loc.at[4])
    ig_copy.start()

    def ig_left():
        ig_copy.wait()
        for a in range(2):
            for n in range(4):
                g_near(n, a).wait_send()
            g_z(z_out.at[a], a).wait_send()

        @pl.when(home)
        def _():
            for n, a in both:
                g_y(n, a).wait_send()

        @pl.when(away)
        def _():
            for a in range(2):
                for n in range(4):
                    g_far(n, a).wait_send()

    drain.append(ig_left)

    @pl.loop(0, PARTS)
    def _(j):
        rows = rows_of(j, n_part)
        step_copy(j).wait_recv()
        step_copy(j).wait_send()
        st[rows, :] = (
            (st[rows, :].astype(F32) + pr[rows, :].astype(F32)) * 0.5
        ).astype(BF16)
        pltpu.make_async_copy(st.at[rows], avg_ref.at[rows], loc.at[5 + j]).start()

    @pl.loop(0, PARTS)
    def _(j):
        rows = rows_of(j, n_part)
        pltpu.make_async_copy(st.at[rows], avg_ref.at[rows], loc.at[5 + j]).wait()

    for left in drain:
        left()


def call_step(level, groups_dp, tokens, gate_weight, up_weight, hidden_grad):
    F, T = tokens.shape
    C, R = gate_weight.shape
    n_part = C // PARTS
    vmem = pltpu.VMEM
    scratch = [
        vmem((2, 2, R, T), BF16),
        vmem((F, T), BF16),
        vmem((2, R, T), BF16),
        vmem((2, 2, T, R), BF16),
        vmem((2, C, R), BF16),
        vmem((2, C, R), BF16),
        vmem((PARTS, 2, R, n_part), BF16),
        vmem((PARTS, 2, R, n_part), BF16),
        vmem((2, C, T), BF16),
        vmem((2, PARTS, 2, n_part, T), F32),
        vmem((2, PARTS, 2, n_part, T), BF16),
        vmem((2, PARTS, 2, n_part, T), BF16),
        vmem((2, C, T), BF16),
        vmem((2, C, T), BF16),
        vmem((C, T), BF16),
        vmem((C, R), BF16),
        vmem((C, R), BF16),
        vmem((C, R), F32),
        vmem((2, 2, R, T), F32),
        vmem((8, F // 2, T), BF16),
        vmem((8, F // 2, T), BF16),
        vmem((8, F // 2, T), BF16),
        vmem((8, F // 2, T), BF16),
        vmem((4, F // 2, T), BF16),
        vmem((4, F // 2, T), BF16),
        vmem((2, F // 2, T), BF16),
        vmem((2, F // 2, T), BF16),
        vmem((F, T), BF16),
        pltpu.SemaphoreType.DMA((SENDS,)),
        pltpu.SemaphoreType.DMA((RECVS,)),
        pltpu.SemaphoreType.DMA((5 + PARTS,)),
    ]
    return pl.pallas_call(
        functools.partial(step_kernel, level, groups_dp),
        out_shape=(
            jax.ShapeDtypeStruct((C, R), BF16),
            jax.ShapeDtypeStruct((F, T), BF16),
        ),
        in_specs=[pl.BlockSpec(memory_space=pl.ANY)] * 4,
        out_specs=[pl.BlockSpec(memory_space=pl.ANY)] * 2,
        scratch_shapes=scratch,
        compiler_params=pltpu.CompilerParams(
            collective_id=level, has_side_effects=True, vmem_limit_bytes=56 * 2**20
        ),
        cost_estimate=pl.CostEstimate(
            flops=20 * T * 8 * F * C, bytes_accessed=6 * R * C, transcendentals=2 * T * C
        ),
    )(tokens, gate_weight, up_weight, hidden_grad)


def shards(tokens, gate_weight, up_weight, hidden_grad, step_index):
    devices = lax.axis_size("dp")
    levels = (devices // 4).bit_length() - 1
    branches = [functools.partial(call_step, level, devices) for level in range(levels)]
    averaged_up, input_grad = lax.switch(
        step_index[0] % levels, branches, tokens.T, gate_weight.T, up_weight.T, hidden_grad.T
    )
    return averaged_up.T, input_grad.T


def solution(mesh):
    placed = (P("dp", "tensor"), P("dp", "tensor"), P("dp", "tensor"), P("dp", "tensor"), P())
    return jax.shard_map(
        shards,
        mesh=mesh,
        in_specs=placed,
        out_specs=(P("dp", "tensor"), P("dp", "tensor")),
        check_vma=False,
    )
```

```python
import functools

import jax
import jax.numpy as jnp
from jax import lax
from jax.experimental import pallas as pl
from jax.experimental.pallas import tpu as pltpu
from jax.sharding import PartitionSpec as P

MESH = pl.DeviceIdType.MESH
BF16, F32 = jnp.bfloat16, jnp.float32
PARTS = 6

X_Z, X_Y, X_FAR, X_NEAR, W_CORE, COT, X_CORE, PART = 0, 2, 6, 14, 22, 24, 25, 27
DELTA, STEP, G_NEAR = PART + 3 * PARTS, PART + 5 * PARTS, PART + 6 * PARTS
G_FAR, G_Y, G_Z, SENDS = G_NEAR + 8, G_NEAR + 16, G_NEAR + 20, G_NEAR + 22
R_X, R_W, R_COT, R_XC, R_PART = 0, 18, 20, 21, 23
R_DELTA, R_STEP, R_NEAR = R_PART + 3 * PARTS, R_PART + 5 * PARTS, R_PART + 6 * PARTS
R_FAR, R_Y, R_Z, RECVS = R_NEAR + 8, R_NEAR + 16, R_NEAR + 20, R_NEAR + 22


def parts_of(level):
    return PARTS if level == 3 else PARTS // 2


def step_kernel(
    level, groups_dp, tok, gw, uw, cot, avg_ref, ig_ref,
    xin, xz, xs, xt, wgb, wub, wgt, wut, hg, pf, sb, rb, ud, us, gd, st, pr,
    ug, acc, near_out, near_in, far_out, far_in, y_out, y_in, z_out, z_in,
    ig_buf, snd, rcv, loc,
):
    F, T = tok.shape
    C, R = gw.shape
    parts = parts_of(level)
    n_part = C // parts
    dp, t = lax.axis_index("dp"), lax.axis_index("tensor")
    core, side = lax.rem(dp, 2), lax.rem(dp // 2, 2)
    x, zh = t // 2, lax.rem(t, 2)
    place = lax.rem(x - 2 * side + 4, 4)
    home = place < 2
    away = place >= 2
    odd = lax.rem(place, 2)
    prim = jnp.where(home, odd, 1 - odd)
    xbit = lax.rem(x, 2)

    sibling = (dp + 1 - 2 * core, t)
    across = (dp + 2 - 4 * side, t)
    anti = (dp, t + 1 - 2 * zh)
    near = (dp, (x + 1 - 2 * xbit) * 2 + zh)
    far = (dp, lax.rem(2 * side + 3 - place, 4) * 2 + zh)
    shift = 4 * 2**level
    target = (lax.rem(dp + shift, groups_dp), t)
    origin = (lax.rem(dp + groups_dp - shift, groups_dp), t)

    partners = [sibling, across, anti, near, far, target]
    if 2 * shift != groups_dp:
        partners.append(origin)
    barrier = pltpu.get_barrier_semaphore()
    for partner in partners:
        pl.semaphore_signal(barrier, inc=1, device_id=partner, device_id_type=MESH)
    pl.semaphore_wait(barrier, len(partners))

    drain = []

    def remote(src, dst, s, r, device):
        return pltpu.make_async_remote_copy(
            src_ref=src, dst_ref=dst, send_sem=snd.at[s], recv_sem=rcv.at[r],
            device_id=device, device_id_type=MESH,
        )

    def rows_of(r, size):
        return pl.ds(pl.multiple_of(r * size, size), size)

    H, Q = F // 2, T // 2

    def half_of(ref, a):
        return ref.at[:, a * Q : (a + 1) * Q]

    def block_of(ref, i, z, y, a):
        return ref.at[i, y, rows_of(z, F), a * Q : (a + 1) * Q]

    def slot(i, z, y, a):
        return ((i * 2 + z) * 2 + y) * 2 + a

    blocks = [(zh, side), (zh, 1 - side), (1 - zh, side), (1 - zh, 1 - side)]

    def to_x(n, a, which, device):
        where = (prim, *blocks[n], a)
        return remote(block_of(xin, *where), block_of(xin, *where), which + 2 * n + a, R_X + slot(*where), device)

    def own_to_x(a, which, device):
        where = (prim, *blocks[0], a)
        return remote(half_of(tok, a), block_of(xin, *where), which + a, R_X + slot(*where), device)

    def x_arrived(i, n, a):
        where = (i, *blocks[n], a)
        remote(half_of(tok, a), block_of(xin, *where), X_Z, R_X + slot(*where), anti).wait_recv()

    mine = (xbit, zh, side)
    later = (xbit, 1 - zh, side)

    def z_home(a):
        return remote(half_of(tok, a), block_of(xin, *mine, a), X_Z + a, R_X + slot(*mine, a), anti)

    def z_away(a):
        return remote(half_of(tok, a), half_of(xz, a), X_Z + a, R_X + 16 + a, anti)

    def y_own(a):
        return remote(half_of(tok, a), block_of(xin, *mine, a), X_Y + a, R_X + slot(*mine, a), across)

    def y_anti(a):
        return remote(half_of(xz, a), block_of(xin, *later, a), X_Y + 2 + a, R_X + slot(*later, a), across)

    own_x = pltpu.make_async_copy(tok, xin.at[xbit, side, rows_of(zh, F)], loc.at[0])
    cot_copy = remote(cot, hg.at[side], COT, R_COT, across)

    @pl.when(home)
    def _():
        for a in range(2):
            z_home(a).start()
            own_to_x(a, X_FAR, far).start()
            own_to_x(a, X_NEAR, near).start()
        own_x.start()
        cot_copy.start()

    @pl.when(away)
    def _():
        for a in range(2):
            z_away(a).start()
            y_own(a).start()

    w_copies = [
        remote(gw, wgb.at[core], W_CORE, R_W, sibling),
        remote(uw, wub.at[core], W_CORE + 1, R_W + 1, sibling),
    ]
    own_copies = [
        pltpu.make_async_copy(gw, wgb.at[core], loc.at[1]),
        pltpu.make_async_copy(uw, wub.at[core], loc.at[2]),
        pltpu.make_async_copy(cot, hg.at[side], loc.at[3]),
    ]
    for copy in own_copies + w_copies:
        copy.start()

    @pl.when(home)
    def _():
        for n, a in ((1, 0), (2, 0), (1, 1), (2, 1)):
            x_arrived(prim, n, a)
            to_x(n, a, X_FAR, far).start()
            to_x(n, a, X_NEAR, near).start()
        own_x.wait()

    @pl.when(away)
    def _():
        def hand_on(n, a):
            x_arrived(prim, n, a)
            to_x(n, a, X_FAR, near).start()

        hand_on(0, 0)
        hand_on(0, 1)
        cot_copy.start()
        for a in range(2):
            z_away(a).wait_recv()
            y_anti(a).start()
            hand_on(1, a)
            hand_on(2, a)

    def forward_last():
        for a in range(2):
            x_arrived(prim, 3, a)

            @pl.when(home)
            def _():
                to_x(3, a, X_FAR, far).start()
                to_x(3, a, X_NEAR, near).start()

            @pl.when(away)
            def _():
                to_x(3, a, X_FAR, near).start()

    for copy in own_copies:
        copy.wait()
    for copy in w_copies:
        copy.wait_recv()
    def x_left():
        cot_copy.wait_send()
        for copy in w_copies:
            copy.wait_send()
        for a in range(2):
            z_home(a).wait_send()
            for n in range(4):
                to_x(n, a, X_FAR, far).wait_send()

        @pl.when(home)
        def _():
            for a in range(2):
                for n in range(4):
                    to_x(n, a, X_NEAR, near).wait_send()

        @pl.when(away)
        def _():
            for a in range(2):
                y_own(a).wait_send()
                y_anti(a).wait_send()

    drain.append(x_left)

    half_y = (1 - side, side)

    def x_copy(y, n):
        return remote(xin.at[1 - core, y], xs.at[y], X_CORE + n, R_XC + n, sibling)

    def sums_copy(h, j, a):
        at = (2 * h + a) * parts + j
        columns = slice(a * Q, (a + 1) * Q) if h == 0 else slice(None)
        view = (h, j, slice(None), slice(None), columns)
        return remote(sb.at[view], rb.at[view], PART + at, R_PART + at, across)

    def halves(h):
        return (0, 1) if h == 0 else (0,)

    def delta_copy(h, j):
        rows = rows_of(j, n_part)
        at = h * parts + j
        return remote(ud.at[h, rows], us.at[h, rows], DELTA + at, R_DELTA + at, sibling)

    def step_copy(j):
        return remote(st.at[rows_of(j, n_part)], pr.at[rows_of(j, n_part)], STEP + j, R_STEP + j, target)

    def sums(h, j, a):
        rows, y = rows_of(j, n_part), half_y[1 - h]
        columns = slice(a * Q, (a + 1) * Q) if h == 0 else slice(None)
        for n, w in ((0, wgb), (1, wub)):
            total = jnp.dot(
                w[0, rows, :], xin[0, y, :, columns], preferred_element_type=F32
            ) + jnp.dot(w[1, rows, :], xin[1, y, :, columns], preferred_element_type=F32)
            pf[h, j, n, :, columns] = total
            sb[h, j, n, :, columns] = total.astype(BF16)

    by_parts = level == 3
    order = [(h, j) for h in range(2) for j in range(parts)]
    if by_parts:
        order = [(h, j) for j in range(parts) for h in range(2)]
    flight = 2 if by_parts else len(order)

    def start_sums(q):
        h, j = order[q]
        for a in halves(h):
            sums_copy(h, j, a).start()

    def next_sums(q):
        h, j = order[q]
        for a in halves(h):
            sums_copy(h, j, a).wait_send()
        if q + flight < len(order):
            start_sums(q + flight)

    for a in range(2):
        x_arrived(1 - prim, 0, a)
        x_arrived(1 - prim, 2, a)

        @pl.loop(0, parts)
        def _(j):
            sums(0, j, a)
            if not by_parts:
                sums_copy(0, j, a).start()

        if by_parts:
            sums_copy(0, 0, a).start()
        if a == 0:
            forward_last()
    x_copy(side, 0).start()
    for n, a in ((1, 0), (1, 1), (3, 0), (3, 1)):
        x_arrived(1 - prim, n, a)
    x_copy(1 - side, 1).start()

    @pl.loop(0, parts)
    def _(j):
        sums(1, j, 0)
        if not by_parts:
            sums_copy(1, j, 0).start()

    if by_parts:
        start_sums(1)

    def sums_left():
        x_copy(side, 0).wait_send()
        x_copy(1 - side, 1).wait_send()
        for h in range(2):
            @pl.loop(0, parts)
            def _(j):
                delta_copy(h, j).wait_send()

    drain.append(sums_left)

    for n, y in ((0, side), (1, 1 - side)):
        xt[1 - n, 0] = xin[core, y].T
        x_copy(y, n).wait_recv()
        xt[1 - n, 1] = xs[y].T
    cot_copy.wait_recv()

    def deltas(h, j):
        y = half_y[h]
        part = rows_of(j, n_part)
        if h == 0:
            for i in range(2):
                wgt[j, i] = wgb[i, part, :].T
                wut[j, i] = wub[i, part, :].T
        next_sums(order.index((h, j)))
        for a in halves(h):
            sums_copy(h, j, a).wait_recv()
        tile = 32 if n_part % 32 == 0 else 16

        @pl.loop(0, n_part // tile)
        def _(r):
            rows = rows_of(r, tile)
            at = pl.ds(pl.multiple_of(j * n_part + r * tile, tile), tile)
            gate = pf[1 - h, j, 0, rows, :] + rb[h, j, 0, rows, :].astype(F32)
            up = pf[1 - h, j, 1, rows, :] + rb[h, j, 1, rows, :].astype(F32)
            sig = 1.0 / (1.0 + jnp.exp(-gate))
            wide = hg[y, at, :].astype(F32)
            ud[h, at, :] = (wide * gate * sig).astype(BF16)
            gd[at, :] = (wide * up * sig * (1.0 + gate * (1.0 - sig))).astype(BF16)

        delta_copy(h, j).start()
        for i in range(2):
            new = jnp.dot(wut[j, i], ud[h, part, :], preferred_element_type=F32) + jnp.dot(
                wgt[j, i], gd[part, :], preferred_element_type=F32
            )
            if j == 0:
                acc[i, y] = new
            else:
                acc[i, y] += new
        delta_copy(h, j).wait_recv()
        grad = jnp.dot(ud[h, part, :], xt[h, 0], preferred_element_type=F32) + jnp.dot(
            us[h, part, :], xt[h, 1], preferred_element_type=F32
        )
        if h == 0:
            ug[part, :] = grad
        else:
            grad += ug[part, :]
            st[part, :] = (wub[core, part, :].astype(F32) - 0.002 * grad).astype(BF16)
            step_copy(j).start()

    pieces = [(1 - zh, 1 - side), (zh, 1 - side), (1 - zh, side), (zh, side)]

    def piece(i, n, a):
        z, y = pieces[n]
        return acc.at[i, y, rows_of(z * 2 + a, H)]

    def g_near(n, a):
        m = 2 * n + a
        return remote(near_out.at[m], near_in.at[m], G_NEAR + m, R_NEAR + m, near)

    def g_far(n, a):
        m = 2 * n + a
        return remote(far_out.at[m], far_in.at[m], G_FAR + m, R_FAR + m, far)

    def g_y(n, a):
        m = 2 * n + a
        return remote(y_out.at[m], y_in.at[m], G_Y + m, R_Y + m, across)

    def g_z(src, a):
        return remote(src, z_in.at[a], G_Z + a, R_Z + a, anti)

    both = [(n, a) for n in range(2) for a in range(2)]

    def nearby(first):
        for n, a in both:
            n = n + first
            near_out[2 * n + a] = piece(1 - prim, n, a)[...].astype(BF16)
            g_near(n, a).start()

    def relay(first):
        @pl.when(away)
        def _():
            for n, a in both:
                n = n + first
                m = 2 * n + a
                g_near(n, a).wait_recv()
                far_out[m] = (piece(prim, n, a)[...] + near_in[m].astype(F32)).astype(BF16)
                g_far(n, a).start()

    def total(n, a):
        g_near(n, a).wait_recv()
        g_far(n, a).wait_recv()
        m = 2 * n + a
        return piece(prim, n, a)[...] + near_in[m].astype(F32) + far_in[m].astype(F32)

    def to_across():
        @pl.when(home)
        def _():
            for n, a in both:
                y_out[2 * n + a] = total(n, a).astype(BF16)
                g_y(n, a).start()

    then = {(0, parts - 1): [lambda: nearby(0)]}
    if not by_parts:
        then[1, 0] = [lambda: relay(0)]
        then[1, parts - 2] = [to_across]
    else:
        then[1, parts - 1] = [lambda: nearby(2), lambda: relay(0), to_across]
    for h, j in order:
        deltas(h, j)
        for step in then.get((h, j), []):
            step()

    if not by_parts:
        nearby(2)
    relay(2)

    @pl.when(away)
    def _():
        for a in range(2):
            g_y(0, a).wait_recv()
            g_z(y_in.at[a], a).start()
        for a in range(2):
            g_y(1, a).wait_recv()
            g_z(z_out.at[a], a).wait_recv()
            ig_buf[rows_of(a, H), :] = (y_in[2 + a].astype(F32) + z_in[a].astype(F32)).astype(BF16)

    @pl.when(home)
    def _():
        for a in range(2):
            z_out[a] = total(2, a).astype(BF16)
            g_z(z_out.at[a], a).start()
        for a in range(2):
            last = total(3, a)
            g_z(z_out.at[a], a).wait_recv()
            ig_buf[rows_of(a, H), :] = (last + z_in[a].astype(F32)).astype(BF16)

    ig_copy = pltpu.make_async_copy(ig_buf, ig_ref, loc.at[4])
    ig_copy.start()

    def ig_left():
        ig_copy.wait()
        for a in range(2):
            for n in range(4):
                g_near(n, a).wait_send()
            g_z(z_out.at[a], a).wait_send()

        @pl.when(home)
        def _():
            for n, a in both:
                g_y(n, a).wait_send()

        @pl.when(away)
        def _():
            for a in range(2):
                for n in range(4):
                    g_far(n, a).wait_send()

    drain.append(ig_left)

    @pl.loop(0, parts)
    def _(j):
        rows = rows_of(j, n_part)
        step_copy(j).wait_recv()
        step_copy(j).wait_send()
        st[rows, :] = (
            (st[rows, :].astype(F32) + pr[rows, :].astype(F32)) * 0.5
        ).astype(BF16)
        pltpu.make_async_copy(st.at[rows], avg_ref.at[rows], loc.at[5 + j]).start()

    @pl.loop(0, parts)
    def _(j):
        rows = rows_of(j, n_part)
        pltpu.make_async_copy(st.at[rows], avg_ref.at[rows], loc.at[5 + j]).wait()

    for left in drain:
        left()


def call_step(level, groups_dp, tokens, gate_weight, up_weight, hidden_grad):
    F, T = tokens.shape
    C, R = gate_weight.shape
    parts = parts_of(level)
    n_part = C // parts
    vmem = pltpu.VMEM
    scratch = [
        vmem((2, 2, R, T), BF16),
        vmem((F, T), BF16),
        vmem((2, R, T), BF16),
        vmem((2, 2, T, R), BF16),
        vmem((2, C, R), BF16),
        vmem((2, C, R), BF16),
        vmem((parts, 2, R, n_part), BF16),
        vmem((parts, 2, R, n_part), BF16),
        vmem((2, C, T), BF16),
        vmem((2, parts, 2, n_part, T), F32),
        vmem((2, parts, 2, n_part, T), BF16),
        vmem((2, parts, 2, n_part, T), BF16),
        vmem((2, C, T), BF16),
        vmem((2, C, T), BF16),
        vmem((C, T), BF16),
        vmem((C, R), BF16),
        vmem((C, R), BF16),
        vmem((C, R), F32),
        vmem((2, 2, R, T), F32),
        vmem((8, F // 2, T), BF16),
        vmem((8, F // 2, T), BF16),
        vmem((8, F // 2, T), BF16),
        vmem((8, F // 2, T), BF16),
        vmem((4, F // 2, T), BF16),
        vmem((4, F // 2, T), BF16),
        vmem((2, F // 2, T), BF16),
        vmem((2, F // 2, T), BF16),
        vmem((F, T), BF16),
        pltpu.SemaphoreType.DMA((SENDS,)),
        pltpu.SemaphoreType.DMA((RECVS,)),
        pltpu.SemaphoreType.DMA((5 + parts,)),
    ]
    return pl.pallas_call(
        functools.partial(step_kernel, level, groups_dp),
        out_shape=(
            jax.ShapeDtypeStruct((C, R), BF16),
            jax.ShapeDtypeStruct((F, T), BF16),
        ),
        in_specs=[pl.BlockSpec(memory_space=pl.ANY)] * 4,
        out_specs=[pl.BlockSpec(memory_space=pl.ANY)] * 2,
        scratch_shapes=scratch,
        compiler_params=pltpu.CompilerParams(
            collective_id=level, has_side_effects=True, vmem_limit_bytes=56 * 2**20
        ),
        cost_estimate=pl.CostEstimate(
            flops=20 * T * 8 * F * C, bytes_accessed=6 * R * C, transcendentals=2 * T * C
        ),
    )(tokens, gate_weight, up_weight, hidden_grad)


def shards(tokens, gate_weight, up_weight, hidden_grad, step_index):
    devices = lax.axis_size("dp")
    levels = (devices // 4).bit_length() - 1
    branches = [functools.partial(call_step, level, devices) for level in range(levels)]
    averaged_up, input_grad = lax.switch(
        step_index[0] % levels, branches, tokens.T, gate_weight.T, up_weight.T, hidden_grad.T
    )
    return averaged_up.T, input_grad.T


def solution(mesh):
    placed = (P("dp", "tensor"), P("dp", "tensor"), P("dp", "tensor"), P("dp", "tensor"), P())
    return jax.shard_map(
        shards,
        mesh=mesh,
        in_specs=placed,
        out_specs=(P("dp", "tensor"), P("dp", "tensor")),
        check_vma=False,
    )
```
